32 devices in a mesh: dp: 2 (over x), expert: 16 (over z, y, core).
Axes of the slice: x: 2, y: 2, z: 4, core: 2. Of those that a mesh axis runs over, the one named last changes fastest.
Arguments:
- routes: int32 [2048, 8], P('expert'), may hold values from 0 to 15, all different within a row; in each aligned block of 128 rows (0 to 127, 128 to 255, ...) at most 80 rows name the same one
- gates: float32 [2048, 8], P('expert'), may hold values from 0.1 to 1
- hidden: bfloat16 [16, 1280, 1024], P('expert', None, 'dp'), may hold values from -6 to 6
- w_down: bfloat16 [16, 1024, 7168], P('expert', None, 'dp'), may hold values from -0.25 to 0.25
- out_grad: bfloat16 [2048, 7168], P('expert', 'dp'), may hold values from -1.5 to 1.5
Outputs:
- mixed: bfloat16 [2048, 7168], P('expert', 'dp')
- hidden_grad: bfloat16 [16, 1280, 1024], P('expert', None, 'dp')
- weight_grad: bfloat16 [16, 1024, 7168], P('expert', None, 'dp')
- gate_grad: float32 [2048, 8], P('expert')
The draws below stay inside these ranges and needn't reach their ends.
Inputs may be any that keep to these rules, and one draw needn't show every extreme that they name: `routes`: each token names 8 different experts; among the 128 tokens held by one device of the expert axis no expert is named more than 80 times, and in every draw some expert is named exactly 80 times by them.
All inputs are finite; a program needn't handle non-finite values.
Results may differ from the reference program's by a relative error of at most 0.014.
Values may be sent and summed in bfloat16 or wider, within the bound.
A program may use at most 128 MiB of HBM per device.

```python
import math
import jax
import jax.numpy as jnp
import numpy as np
from jax import lax

D = 7168
HIDDEN_SIZE = 1024
TOPK = 8
TOK_DEV = 128
EXPERTS = 16
CAP = 80
TOKENS = 2048
SLOTS = 1280
WBLOCK = 3584
N_DP = 2
N_EXPERT = 16


def with_spikes(entries, own_key, source, target, blocks, factor):
    owner, partner = [(jnp.arange(entries.shape[axis_at]) // (entries.shape[axis_at] // blocks)).reshape([-1 if axis == axis_at else 1 for axis in range(entries.ndim)]) for axis_at in (source, target)]
    chosen = jax.random.permutation(own_key, blocks)[partner]
    strong = (owner == chosen) | (owner == (partner + blocks // 2) % blocks)
    return jnp.where(strong, factor * entries, entries)


def level_of(rng, dims, split, low, high):
    level, own = 1.0, jax.random.fold_in(rng, 6)
    for dim, parts in split:
        steps = jnp.exp(jax.random.uniform(jax.random.fold_in(own, dim), (parts,), jnp.float32, low / len(split), high / len(split)))
        level = level * jnp.repeat(steps, dims[dim] // parts).reshape([-1 if axis == dim else 1 for axis in range(len(dims))])
    return level


def routed_block(stream_key, own, number, rows, number_of, top, limit, skew):
    ranking = jax.random.permutation(stream_key, number_of)
    crowded, common = shares(number_of, rows * top, limit, skew, True), shares(number_of, rows * top, limit, skew, False)
    places = jnp.arange(number_of)

    def named(lengths, rotation):
        used = int((lengths > 0).sum())
        fixed = max(1, used // 4)
        passed = fixed + (places - fixed + rotation * (used - fixed)) % max(1, number_of - fixed)
        return jnp.zeros((number_of,), jnp.int32).at[ranking[jnp.where(places < fixed, places, passed)]].set(jnp.asarray(lengths, jnp.int32))

    lengths = jnp.where(number % 4 == 0, named(crowded, number // 4), named(common, number - number // 4 - 1))
    mixed = jax.random.permutation(jax.random.fold_in(own, 3), number_of)
    source_of, sink = mixed[0:number_of // 2 * 2:2], mixed[1:number_of // 2 * 2:2]
    slack = jnp.minimum(lengths[source_of] - 1, limit - lengths[sink]) // 2
    slack = jnp.where((source_of == ranking[0]) | (sink == ranking[0]) | (lengths[sink] == 0), 0, jnp.maximum(slack, 0))
    passed = jax.random.randint(jax.random.fold_in(own, 4), (number_of // 2,), 0, 1 << 20) % (slack + 1)
    lengths = lengths.at[source_of].add(-passed).at[sink].add(passed)
    labels = jnp.searchsorted(jnp.cumsum(lengths), jnp.arange(rows * top), side="right").astype(jnp.int32)
    table = labels.reshape(top, rows).T
    table = table[jax.random.permutation(jax.random.fold_in(own, 1), rows)]
    rotation = jax.random.randint(jax.random.fold_in(own, 2), (rows, 1), 0, top)
    return jnp.take_along_axis(table, (jnp.arange(top)[None, :] + rotation) % top, axis=1)


def shares(count, total, most, lean, full):
    weights = [(1 << 20) // math.isqrt(standing ** lean) + 1 for standing in range(1, count + 1)]
    largest = most if full else min(most, max(-(-total // count), total * weights[0] // sum(weights)))
    least = 1 if total - largest >= count - 1 else 0
    counts, rest = [largest] + [least] * (count - 1), total - largest - least * (count - 1)
    while rest > 0:
        candidates = [i for i in range(1, count) if counts[i] < largest] or [i for i in range(1, count) if counts[i] < most]
        whole, remaining = sum([weights[i] for i in candidates]), rest
        for i in candidates:
            extra = min(most - counts[i], max(1, remaining * weights[i] // whole), rest)
            counts[i] = counts[i] + extra
            rest = rest - extra
    return np.array(counts)


def gaussian(rng, extent, width, bound, pieces=(), kind=jnp.bfloat16):
    drawn = width * jax.random.normal(rng, extent, jnp.float32)
    if pieces:
        drawn = drawn * level_of(rng, extent, pieces, -0.22, 0.18)
    return jnp.clip(drawn, -bound, bound).astype(kind)


def heavy_noise(key, extent, width, bound, pieces, heavy, kind=jnp.bfloat16):
    array = width * jax.random.normal(key, extent, jnp.float32)
    if pieces:
        array = array * level_of(key, extent, pieces, -0.22, 0.18)
    return jnp.clip(with_spikes(array, jax.random.fold_in(key, 3), *heavy), -bound, bound).astype(kind)


def setup_inputs(seed: int = 0) -> dict:
    arg_keys = jax.random.split(jax.random.key(seed), 6)
    routes_keys = jax.random.split(jax.random.fold_in(arg_keys[0], 1), TOKENS // TOK_DEV)
    routes_turns = jax.random.permutation(jax.random.fold_in(arg_keys[0], 3), TOKENS // TOK_DEV)
    routes = jax.vmap(lambda own, number: routed_block(jax.random.fold_in(arg_keys[0], 2), own, number, TOK_DEV, EXPERTS, TOPK, CAP, 2))(routes_keys, routes_turns).reshape((TOKENS, TOPK))
    gates = jnp.clip(jnp.exp(math.log(1.0) - 2.3025851 * jax.random.uniform(arg_keys[1], (TOKENS, TOPK), jnp.float32) ** level_of(arg_keys[1], (TOKENS, TOPK), ((0, 16),), -0.2, 0.2)), 0.1, 1.0)
    hidden = gaussian(arg_keys[2], (EXPERTS, SLOTS, HIDDEN_SIZE), 1.0, 6.0, ((0, 16), (2, 2)))
    w_down = heavy_noise(arg_keys[3], (EXPERTS, HIDDEN_SIZE, D), HIDDEN_SIZE ** -0.5, 0.25, ((0, 16), (2, 2)), (2, 1, 2, 2.0))
    out_grad = gaussian(arg_keys[4], (TOKENS, D), 0.25, 1.5, ((0, 16), (1, 2)))
    return {"routes": routes, "gates": gates, "hidden": hidden, "w_down": w_down, "out_grad": out_grad}


def reference(routes, gates, hidden, w_down, out_grad):
    flat = routes.reshape(N_EXPERT, TOK_DEV * TOPK)
    onehot = (flat[:, :, None] == jnp.arange(EXPERTS, dtype=jnp.int32)[None, None, :]).astype(jnp.int32)
    before = jnp.cumsum(onehot, axis=1) - onehot
    rank = jnp.sum(before * onehot, axis=2)
    offset = jnp.arange(N_EXPERT, dtype=jnp.int32)[:, None] * CAP
    slot = (rank + offset).reshape(TOKENS, TOPK).astype(jnp.int32)
    grad_wide = out_grad.astype(jnp.float32)

    def per_expert(carry, inputs):
        mixed_acc, gate_acc = carry
        index, h_e, w_e = inputs
        out_e = jnp.dot(h_e, w_e, preferred_element_type=jnp.float32).astype(jnp.bfloat16)
        chosen = routes == index
        weight = jnp.sum(jnp.where(chosen, gates, jnp.float32(0.0)), axis=1)
        where_slot = jnp.sum(jnp.where(chosen, slot, 0), axis=1).astype(jnp.int32)
        taken = jnp.any(chosen, axis=1)
        rows = jnp.take(out_e, where_slot, axis=0).astype(jnp.float32)
        mixed_acc = mixed_acc + weight[:, None] * rows
        dots = jnp.sum(grad_wide * rows, axis=1)
        gate_acc = gate_acc + jnp.where(chosen, dots[:, None], jnp.float32(0.0))
        target = jnp.where(taken, where_slot, SLOTS).astype(jnp.int32)
        values = (weight[:, None] * grad_wide).astype(jnp.bfloat16)
        grad_e = jnp.zeros((SLOTS, D), jnp.bfloat16).at[target].set(values, mode="drop")
        wgrad = lax.dot_general(h_e, grad_e, (((0,), (0,)), ((), ())), preferred_element_type=jnp.float32).astype(jnp.bfloat16)
        blocks = jnp.einsum("sbd,hbd->bsh", grad_e.reshape(SLOTS, N_DP, WBLOCK).astype(jnp.float32), w_e.reshape(HIDDEN_SIZE, N_DP, WBLOCK).astype(jnp.float32))
        blocks = lax.optimization_barrier(blocks.astype(jnp.bfloat16)).astype(jnp.float32)
        hgrad = jnp.sum(blocks, axis=0).astype(jnp.bfloat16)
        return (mixed_acc, gate_acc), (hgrad, wgrad)

    start = (jnp.zeros((TOKENS, D), jnp.float32), jnp.zeros((TOKENS, TOPK), jnp.float32))
    experts_index = jnp.arange(EXPERTS, dtype=jnp.int32)
    (mixed_acc, gate_acc), (hidden_grad, weight_grad) = lax.scan(per_expert, start, (experts_index, hidden, w_down))
    return mixed_acc.astype(jnp.bfloat16), hidden_grad, weight_grad, gate_acc
```

```python
import jax
import jax.numpy as jnp
from jax import lax
from jax.sharding import PartitionSpec as P

CHUNKS = 2


def swap(x):
    return lax.ppermute(x, "dp", [(0, 1), (1, 0)])


def per_device(routes, gates, hidden, w_down, out_grad):
    experts = lax.axis_size("expert")
    n_dp = lax.axis_size("dp")
    dp = lax.axis_index("dp")
    h_local = hidden[0]
    w_local = w_down[0]
    slots, part = h_local.shape
    cap = slots // experts
    width = w_local.shape[1]
    tok = routes.shape[0]
    large = experts * tok > 4096
    chunks = 4 if large else CHUNKS
    step = width // chunks

    named = routes[None] == jnp.arange(experts, dtype=jnp.int32)[:, None, None]
    dense = jnp.max(jnp.where(named, gates[None], jnp.float32(-1.0)), axis=2)
    mine = lax.all_to_all(dense, "expert", split_axis=0, concat_axis=0, tiled=True)
    taken = mine >= 0
    earlier = (jnp.arange(tok)[:, None] < jnp.arange(tok)[None, :]).astype(jnp.bfloat16)
    rank = jnp.dot(taken.astype(jnp.bfloat16), earlier, preferred_element_type=jnp.float32)
    rank = jnp.where(taken, rank, -1.0).astype(jnp.int32)
    pick = rank[:, None, :] == jnp.arange(cap, dtype=jnp.int32)[None, :, None]
    slot_gate = jnp.sum(jnp.where(pick, mine[:, None, :], 0.0), axis=2)[:, :, None]
    sel = pick.astype(jnp.bfloat16)

    if n_dp == 2:
        other = swap(h_local)
        whole = jnp.where(
            dp == 0,
            jnp.concatenate([h_local, other], axis=1),
            jnp.concatenate([other, h_local], axis=1),
        )
    else:
        whole = lax.all_gather(h_local, "dp", axis=1, tiled=True)

    mixed, weight_grad = [], []
    partial_hidden = jnp.zeros((slots, whole.shape[1]), jnp.float32)
    dots = jnp.zeros((experts, cap), jnp.float32)
    for c in range(chunks):
        grad_c = out_grad[:, c * step : (c + 1) * step]
        w_c = w_local[:, c * step : (c + 1) * step]
        if large and c:
            grad_c, w_c, partial_hidden, dots, mixed[-1] = lax.optimization_barrier(
                (grad_c, w_c, partial_hidden, dots, mixed[-1])
            )
        og = lax.all_gather(grad_c, "expert", axis=0, tiled=True).reshape(experts, tok, step)
        out = jnp.dot(whole, w_c, preferred_element_type=jnp.float32).astype(jnp.bfloat16)
        out = out.reshape(experts, cap, step)
        scaled = (slot_gate * out.astype(jnp.float32)).astype(jnp.bfloat16)
        share = jnp.einsum(
            "jrt,jrc->jtc", sel, scaled, preferred_element_type=jnp.float32
        ).astype(jnp.bfloat16)
        mixed.append(
            lax.psum_scatter(
                share.reshape(experts * tok, step), "expert", scatter_dimension=0, tiled=True
            )
        )
        rows = jnp.einsum(
            "jrt,jtc->jrc", sel, og, preferred_element_type=jnp.float32
        ).astype(jnp.bfloat16)
        rows = rows.astype(jnp.float32)
        dots = dots + jnp.sum(rows * out.astype(jnp.float32), axis=2)
        grad_slots = (slot_gate * rows).astype(jnp.bfloat16).reshape(slots, step)
        weight_grad.append(
            lax.dot_general(
                whole, grad_slots, (((0,), (0,)), ((), ())), preferred_element_type=jnp.float32
            ).astype(jnp.bfloat16)
        )
        partial_hidden = partial_hidden + lax.dot_general(
            grad_slots, w_c, (((1,), (1,)), ((), ())), preferred_element_type=jnp.float32
        )
    by_token = jnp.sum(jnp.where(pick, dots[:, :, None], 0.0), axis=1)
    back = lax.all_to_all(by_token, "expert", split_axis=0, concat_axis=0, tiled=True)
    gate_part = jnp.sum(jnp.where(named, back[:, :, None], 0.0), axis=0)
    rounded = partial_hidden.astype(jnp.bfloat16)
    if n_dp == 2:
        gate_grad = gate_part + swap(gate_part)
        keep = lax.dynamic_slice_in_dim(rounded, dp * part, part, axis=1)
        give = lax.dynamic_slice_in_dim(rounded, (1 - dp) * part, part, axis=1)
        hidden_grad = (keep.astype(jnp.float32) + swap(give).astype(jnp.float32)).astype(jnp.bfloat16)
    else:
        gate_grad = lax.psum(gate_part, "dp")
        hidden_grad = lax.psum_scatter(rounded, "dp", scatter_dimension=1, tiled=True)
    mixed = jnp.concatenate(mixed, axis=1)
    weight_grad = jnp.concatenate(weight_grad, axis=1)
    return (mixed, hidden_grad[None], weight_grad[None], gate_grad)


def solution(mesh):
    in_specs = (
        P("expert", None),
        P("expert", None),
        P("expert", None, "dp"),
        P("expert", None, "dp"),
        P("expert", "dp"),
    )
    out_specs = (
        P("expert", "dp"),
        P("expert", None, "dp"),
        P("expert", None, "dp"),
        P("expert", None),
    )
    return jax.shard_map(
        per_device, mesh=mesh, in_specs=in_specs, out_specs=out_specs, check_vma=False
    )
```

```python
import jax
import jax.numpy as jnp
from jax import lax
from jax.sharding import PartitionSpec as P

CHUNKS = 2


def swap(x):
    return lax.ppermute(x, "dp", [(0, 1), (1, 0)])


def place(sel, rows):
    return jnp.einsum(
        "jrt,jrc->jtc", sel, rows, preferred_element_type=jnp.float32
    ).astype(jnp.bfloat16)


def take(sel, tokens):
    return jnp.einsum(
        "jrt,jtc->jrc", sel, tokens, preferred_element_type=jnp.float32
    ).astype(jnp.bfloat16)


def per_device(routes, gates, hidden, w_down, out_grad):
    experts = lax.axis_size("expert")
    n_dp = lax.axis_size("dp")
    dp = lax.axis_index("dp")
    h_local = hidden[0]
    w_local = w_down[0]
    slots, part = h_local.shape
    cap = slots // experts
    width = w_local.shape[1]
    tok = routes.shape[0]
    large = experts * tok > 4096
    paired = experts % 2 == 0 and not large
    half = experts // 2
    core = lax.axis_index("expert") % 2
    across = [(i, i ^ 1) for i in range(experts)]
    alike = [list(range(p, experts, 2)) for p in range(2)]

    def own_first(x):
        pairs = x.reshape((half, 2) + x.shape[1:])
        even, odd = pairs[:, 0], pairs[:, 1]
        return jnp.concatenate(
            [jnp.where(core == 0, even, odd), jnp.where(core == 0, odd, even)], axis=0
        )

    def in_order(x):
        own, other = x[:half], x[half:]
        pairs = jnp.stack(
            [jnp.where(core == 0, own, other), jnp.where(core == 0, other, own)], axis=1
        )
        return pairs.reshape(x.shape)

    chunks = 4 if large else CHUNKS
    step = width // chunks

    named = routes[None] == jnp.arange(experts, dtype=jnp.int32)[:, None, None]
    dense = jnp.max(jnp.where(named, gates[None], jnp.float32(-1.0)), axis=2)
    mine = lax.all_to_all(dense, "expert", split_axis=0, concat_axis=0, tiled=True)
    if paired:
        mine = own_first(mine)
        h_local = own_first(h_local.reshape(experts, cap, part)).reshape(slots, part)
    taken = mine >= 0
    earlier = (jnp.arange(tok)[:, None] < jnp.arange(tok)[None, :]).astype(jnp.bfloat16)
    rank = jnp.dot(taken.astype(jnp.bfloat16), earlier, preferred_element_type=jnp.float32)
    rank = jnp.where(taken, rank, -1.0).astype(jnp.int32)
    pick = rank[:, None, :] == jnp.arange(cap, dtype=jnp.int32)[None, :, None]
    slot_gate = jnp.sum(jnp.where(pick, mine[:, None, :], 0.0), axis=2)[:, :, None]
    sel = pick.astype(jnp.bfloat16)

    if n_dp == 2:
        other = swap(h_local)
        whole = jnp.where(
            dp == 0,
            jnp.concatenate([h_local, other], axis=1),
            jnp.concatenate([other, h_local], axis=1),
        )
    else:
        whole = lax.all_gather(h_local, "dp", axis=1, tiled=True)

    mixed, weight_grad = [], []
    partial_hidden = jnp.zeros((slots, whole.shape[1]), jnp.float32)
    dots = jnp.zeros((experts, cap), jnp.float32)
    for c in range(chunks):
        grad_c = out_grad[:, c * step : (c + 1) * step]
        w_c = w_local[:, c * step : (c + 1) * step]
        if large and c:
            grad_c, w_c, partial_hidden, dots, mixed[-1] = lax.optimization_barrier(
                (grad_c, w_c, partial_hidden, dots, mixed[-1])
            )
        out = jnp.dot(whole, w_c, preferred_element_type=jnp.float32).astype(jnp.bfloat16)
        out = out.reshape(experts, cap, step)
        scaled = (slot_gate * out.astype(jnp.float32)).astype(jnp.bfloat16)
        if paired:
            near = lax.all_gather(
                grad_c, "expert", axis=0, tiled=True, axis_index_groups=alike
            )
            far = lax.ppermute(near, "expert", across)
            give = place(sel[half:], scaled[half:])
            got = lax.ppermute(give, "expert", across)
            share = place(sel[:half], scaled[:half]).astype(jnp.float32) + got.astype(jnp.float32)
            share = share.astype(jnp.bfloat16).reshape(half * tok, step)
            mixed.append(
                lax.psum_scatter(
                    share, "expert", scatter_dimension=0, tiled=True, axis_index_groups=alike
                )
            )
            rows = jnp.concatenate(
                [
                    take(sel[:half], near.reshape(half, tok, step)),
                    take(sel[half:], far.reshape(half, tok, step)),
                ],
                axis=0,
            )
        else:
            og = lax.all_gather(grad_c, "expert", axis=0, tiled=True)
            share = place(sel, scaled).reshape(experts * tok, step)
            mixed.append(lax.psum_scatter(share, "expert", scatter_dimension=0, tiled=True))
            rows = take(sel, og.reshape(experts, tok, step))
        rows = rows.astype(jnp.float32)
        dots = dots + jnp.sum(rows * out.astype(jnp.float32), axis=2)
        grad_slots = (slot_gate * rows).astype(jnp.bfloat16).reshape(slots, step)
        weight_grad.append(
            lax.dot_general(
                whole, grad_slots, (((0,), (0,)), ((), ())), preferred_element_type=jnp.float32
            ).astype(jnp.bfloat16)
        )
        partial_hidden = partial_hidden + lax.dot_general(
            grad_slots, w_c, (((1,), (1,)), ((), ())), preferred_element_type=jnp.float32
        )
    by_token = jnp.sum(jnp.where(pick, dots[:, :, None], 0.0), axis=1)
    if paired:
        by_token = in_order(by_token)
    back = lax.all_to_all(by_token, "expert", split_axis=0, concat_axis=0, tiled=True)
    gate_part = jnp.sum(jnp.where(named, back[:, :, None], 0.0), axis=0)
    rounded = partial_hidden.astype(jnp.bfloat16)
    if n_dp == 2:
        gate_grad = gate_part + swap(gate_part)
        keep = lax.dynamic_slice_in_dim(rounded, dp * part, part, axis=1)
        give = lax.dynamic_slice_in_dim(rounded, (1 - dp) * part, part, axis=1)
        hidden_grad = (keep.astype(jnp.float32) + swap(give).astype(jnp.float32)).astype(jnp.bfloat16)
    else:
        gate_grad = lax.psum(gate_part, "dp")
        hidden_grad = lax.psum_scatter(rounded, "dp", scatter_dimension=1, tiled=True)
    mixed = jnp.concatenate(mixed, axis=1)
    weight_grad = jnp.concatenate(weight_grad, axis=1)
    if paired:
        hidden_grad = in_order(hidden_grad.reshape(experts, cap, part)).reshape(slots, part)
    return (mixed, hidden_grad[None], weight_grad[None], gate_grad)


def solution(mesh):
    in_specs = (
        P("expert", None),
        P("expert", None),
        P("expert", None, "dp"),
        P("expert", None, "dp"),
        P("expert", "dp"),
    )
    out_specs = (
        P("expert", "dp"),
        P("expert", None, "dp"),
        P("expert", None, "dp"),
        P("expert", None),
    )
    return jax.shard_map(
        per_device, mesh=mesh, in_specs=in_specs, out_specs=out_specs, check_vma=False
    )
```

```python
import jax
import jax.numpy as jnp
from jax import lax
from jax.sharding import PartitionSpec as P

CHUNKS = 2


def swap(x):
    return lax.ppermute(x, "dp", [(0, 1), (1, 0)])


def gather_tokens(x, large):
    n = lax.axis_size("expert")
    if large or n % 4:
        return lax.all_gather(x, "expert", axis=0, tiled=True)
    me = lax.axis_index("expert")
    quads = n // 4
    held = jnp.zeros((quads,) + x.shape, x.dtype)
    for s in range(quads):
        block = lax.ppermute(x, "expert", [(i, (i + 4 * s) % n) for i in range(n)]) if s else x
        held = lax.dynamic_update_index_in_dim(held, block, (me // 4 - s) % quads, 0)
    for axis, bit in ((1, 2), (2, 1)):
        other = lax.ppermute(held, "expert", [(i, i ^ bit) for i in range(n)])
        held = jnp.where(
            (me // bit) % 2 == 0,
            jnp.stack([held, other], axis=axis),
            jnp.stack([other, held], axis=axis),
        )
    return held


def per_device(routes, gates, hidden, w_down, out_grad):
    experts = lax.axis_size("expert")
    n_dp = lax.axis_size("dp")
    dp = lax.axis_index("dp")
    h_local = hidden[0]
    w_local = w_down[0]
    slots, part = h_local.shape
    cap = slots // experts
    width = w_local.shape[1]
    tok = routes.shape[0]
    large = experts * tok > 4096
    chunks = 4 if large else CHUNKS
    step = width // chunks

    named = routes[None] == jnp.arange(experts, dtype=jnp.int32)[:, None, None]
    dense = jnp.max(jnp.where(named, gates[None], jnp.float32(-1.0)), axis=2)
    mine = lax.all_to_all(dense, "expert", split_axis=0, concat_axis=0, tiled=True)
    taken = mine >= 0
    earlier = (jnp.arange(tok)[:, None] < jnp.arange(tok)[None, :]).astype(jnp.bfloat16)
    rank = jnp.dot(taken.astype(jnp.bfloat16), earlier, preferred_element_type=jnp.float32)
    rank = jnp.where(taken, rank, -1.0).astype(jnp.int32)
    pick = rank[:, None, :] == jnp.arange(cap, dtype=jnp.int32)[None, :, None]
    slot_gate = jnp.sum(jnp.where(pick, mine[:, None, :], 0.0), axis=2)[:, :, None]
    sel = pick.astype(jnp.bfloat16)

    if n_dp == 2:
        other = swap(h_local)
        whole = jnp.where(
            dp == 0,
            jnp.concatenate([h_local, other], axis=1),
            jnp.concatenate([other, h_local], axis=1),
        )
    else:
        whole = lax.all_gather(h_local, "dp", axis=1, tiled=True)

    mixed, weight_grad = [], []
    partial_hidden = jnp.zeros((slots, whole.shape[1]), jnp.float32)
    dots = jnp.zeros((experts, cap), jnp.float32)
    for c in range(chunks):
        grad_c = out_grad[:, c * step : (c + 1) * step]
        w_c = w_local[:, c * step : (c + 1) * step]
        if large and c:
            grad_c, w_c, partial_hidden, dots, mixed[-1] = lax.optimization_barrier(
                (grad_c, w_c, partial_hidden, dots, mixed[-1])
            )
        og = gather_tokens(grad_c, large).reshape(experts, tok, step)
        out = jnp.dot(whole, w_c, preferred_element_type=jnp.float32).astype(jnp.bfloat16)
        out = out.reshape(experts, cap, step)
        scaled = (slot_gate * out.astype(jnp.float32)).astype(jnp.bfloat16)
        share = jnp.einsum(
            "jrt,jrc->jtc", sel, scaled, preferred_element_type=jnp.float32
        ).astype(jnp.bfloat16)
        mixed.append(
            lax.psum_scatter(
                share.reshape(experts * tok, step), "expert", scatter_dimension=0, tiled=True
            )
        )
        rows = jnp.einsum(
            "jrt,jtc->jrc", sel, og, preferred_element_type=jnp.float32
        ).astype(jnp.bfloat16)
        rows = rows.astype(jnp.float32)
        dots = dots + jnp.sum(rows * out.astype(jnp.float32), axis=2)
        grad_slots = (slot_gate * rows).astype(jnp.bfloat16).reshape(slots, step)
        weight_grad.append(
            lax.dot_general(
                whole, grad_slots, (((0,), (0,)), ((), ())), preferred_element_type=jnp.float32
            ).astype(jnp.bfloat16)
        )
        partial_hidden = partial_hidden + lax.dot_general(
            grad_slots, w_c, (((1,), (1,)), ((), ())), preferred_element_type=jnp.float32
        )
    by_token = jnp.sum(jnp.where(pick, dots[:, :, None], 0.0), axis=1)
    back = lax.all_to_all(by_token, "expert", split_axis=0, concat_axis=0, tiled=True)
    gate_part = jnp.sum(jnp.where(named, back[:, :, None], 0.0), axis=0)
    rounded = partial_hidden.astype(jnp.bfloat16)
    if n_dp == 2:
        gate_grad = gate_part + swap(gate_part)
        keep = lax.dynamic_slice_in_dim(rounded, dp * part, part, axis=1)
        give = lax.dynamic_slice_in_dim(rounded, (1 - dp) * part, part, axis=1)
        hidden_grad = (keep.astype(jnp.float32) + swap(give).astype(jnp.float32)).astype(jnp.bfloat16)
    else:
        gate_grad = lax.psum(gate_part, "dp")
        hidden_grad = lax.psum_scatter(rounded, "dp", scatter_dimension=1, tiled=True)
    mixed = jnp.concatenate(mixed, axis=1)
    weight_grad = jnp.concatenate(weight_grad, axis=1)
    return (mixed, hidden_grad[None], weight_grad[None], gate_grad)


def solution(mesh):
    in_specs = (
        P("expert", None),
        P("expert", None),
        P("expert", None, "dp"),
        P("expert", None, "dp"),
        P("expert", "dp"),
    )
    out_specs = (
        P("expert", "dp"),
        P("expert", None, "dp"),
        P("expert", None, "dp"),
        P("expert", None),
    )
    return jax.shard_map(
        per_device, mesh=mesh, in_specs=in_specs, out_specs=out_specs, check_vma=False
    )
```

```python
import jax
import jax.numpy as jnp
from jax import lax
from jax.sharding import PartitionSpec as P

CHUNKS = 1


def swap(x):
    return lax.ppermute(x, "dp", [(0, 1), (1, 0)])


def per_device(routes, gates, hidden, w_down, out_grad):
    experts = lax.axis_size("expert")
    n_dp = lax.axis_size("dp")
    dp = lax.axis_index("dp")
    h_local = hidden[0]
    w_local = w_down[0]
    slots, part = h_local.shape
    cap = slots // experts
    width = w_local.shape[1]
    tok = routes.shape[0]
    large = experts * tok > 4096
    chunks = 4 if large else CHUNKS
    step = width // chunks

    named = routes[None] == jnp.arange(experts, dtype=jnp.int32)[:, None, None]
    dense = jnp.max(jnp.where(named, gates[None], jnp.float32(-1.0)), axis=2)
    mine = lax.all_to_all(dense, "expert", split_axis=0, concat_axis=0, tiled=True)
    taken = mine >= 0
    earlier = (jnp.arange(tok)[:, None] < jnp.arange(tok)[None, :]).astype(jnp.bfloat16)
    rank = jnp.dot(taken.astype(jnp.bfloat16), earlier, preferred_element_type=jnp.float32)
    rank = jnp.where(taken, rank, -1.0).astype(jnp.int32)
    pick = rank[:, None, :] == jnp.arange(cap, dtype=jnp.int32)[None, :, None]
    slot_gate = jnp.sum(jnp.where(pick, mine[:, None, :], 0.0), axis=2)[:, :, None]
    sel = pick.astype(jnp.bfloat16)

    if n_dp == 2:
        other = swap(h_local)
        whole = jnp.where(
            dp == 0,
            jnp.concatenate([h_local, other], axis=1),
            jnp.concatenate([other, h_local], axis=1),
        )
    else:
        whole = lax.all_gather(h_local, "dp", axis=1, tiled=True)

    mixed, weight_grad = [], []
    partial_hidden = jnp.zeros((slots, whole.shape[1]), jnp.float32)
    dots = jnp.zeros((experts, cap), jnp.float32)
    for c in range(chunks):
        grad_c = out_grad[:, c * step : (c + 1) * step]
        w_c = w_local[:, c * step : (c + 1) * step]
        if large and c:
            grad_c, w_c, partial_hidden, dots, mixed[-1] = lax.optimization_barrier(
                (grad_c, w_c, partial_hidden, dots, mixed[-1])
            )
        og = lax.all_gather(grad_c, "expert", axis=0, tiled=True).reshape(experts, tok, step)
        out = jnp.dot(whole, w_c, preferred_element_type=jnp.float32).astype(jnp.bfloat16)
        out = out.reshape(experts, cap, step)
        scaled = (slot_gate * out.astype(jnp.float32)).astype(jnp.bfloat16)
        share = jnp.einsum(
            "jrt,jrc->jtc", sel, scaled, preferred_element_type=jnp.float32
        ).astype(jnp.bfloat16)
        mixed.append(
            lax.psum_scatter(
                share.reshape(experts * tok, step), "expert", scatter_dimension=0, tiled=True
            )
        )
        rows = jnp.einsum(
            "jrt,jtc->jrc", sel, og, preferred_element_type=jnp.float32
        ).astype(jnp.bfloat16)
        rows = rows.astype(jnp.float32)
        dots = dots + jnp.sum(rows * out.astype(jnp.float32), axis=2)
        grad_slots = (slot_gate * rows).astype(jnp.bfloat16).reshape(slots, step)
        weight_grad.append(
            lax.dot_general(
                whole, grad_slots, (((0,), (0,)), ((), ())), preferred_element_type=jnp.float32
            ).astype(jnp.bfloat16)
        )
        partial_hidden = partial_hidden + lax.dot_general(
            grad_slots, w_c, (((1,), (1,)), ((), ())), preferred_element_type=jnp.float32
        )
    by_token = jnp.sum(jnp.where(pick, dots[:, :, None], 0.0), axis=1)
    back = lax.all_to_all(by_token, "expert", split_axis=0, concat_axis=0, tiled=True)
    gate_part = jnp.sum(jnp.where(named, back[:, :, None], 0.0), axis=0)
    rounded = partial_hidden.astype(jnp.bfloat16)
    if n_dp == 2:
        gate_grad = gate_part + swap(gate_part)
        keep = lax.dynamic_slice_in_dim(rounded, dp * part, part, axis=1)
        give = lax.dynamic_slice_in_dim(rounded, (1 - dp) * part, part, axis=1)
        hidden_grad = (keep.astype(jnp.float32) + swap(give).astype(jnp.float32)).astype(jnp.bfloat16)
    else:
        gate_grad = lax.psum(gate_part, "dp")
        hidden_grad = lax.psum_scatter(rounded, "dp", scatter_dimension=1, tiled=True)
    mixed = jnp.concatenate(mixed, axis=1)
    weight_grad = jnp.concatenate(weight_grad, axis=1)
    return (mixed, hidden_grad[None], weight_grad[None], gate_grad)


def solution(mesh):
    in_specs = (
        P("expert", None),
        P("expert", None),
        P("expert", None, "dp"),
        P("expert", None, "dp"),
        P("expert", "dp"),
    )
    out_specs = (
        P("expert", "dp"),
        P("expert", None, "dp"),
        P("expert", None, "dp"),
        P("expert", None),
    )
    return jax.shard_map(
        per_device, mesh=mesh, in_specs=in_specs, out_specs=out_specs, check_vma=False
    )
```
